32 devices in a mesh: chan: 8 (over z, x), band: 4 (over y, core).
Axes of the slice: x: 2, y: 2, z: 4, core: 2. Of those that a mesh axis runs over, the one named last changes fastest.
Arguments:
- spectra: float32 [2, 32, 96, 1024], P(None, None, 'band', 'chan'), may hold values from -6 to 6
- taps: float32 [96, 16], replicated, may hold values from -2.5 to 2.5
Outputs:
- stacked: bfloat16 [8, 2, 1024, 1024], P('band', None, 'chan')
The draws below stay inside these ranges and needn't reach their ends.
All inputs are finite; a program needn't handle non-finite values.
Results may differ from the reference program's by a relative error of at most 0.0057.
Values may be sent and summed in bfloat16 or wider, within the bound.
A program may use at most 192 MiB of HBM per device.

```python
import jax
import jax.numpy as jnp
from jax import lax

W = 32
F = 96
BANDS = 8
TAPS = 16
SMOOTH = 5
BAND_BINS = 12
CHANNELS = 1024


def block_scale(rng, shape, split, smallest, top_value):
    def one(position, shards_of):
        heights = jax.random.uniform(jax.random.fold_in(jax.random.fold_in(rng, 6), position), (shards_of,), jnp.float32, smallest / len(split), top_value / len(split))
        return jnp.repeat(jnp.exp(heights), shape[position] // shards_of).reshape((-1,) + (1,) * (len(shape) - position - 1))

    gain = one(*split[0])
    for cut in split[1:]:
        gain = gain * one(*cut)
    return gain


def normal_values(own_key, extent, spread, most, shards=(), dtype=jnp.bfloat16):
    values = jax.random.normal(own_key, extent, jnp.float32) * spread
    if len(shards) > 0:
        values = block_scale(own_key, extent, shards, -0.22, 0.18) * values
    return jnp.clip(values, min=-most, max=most).astype(dtype)


def setup_inputs(seed: int = 0) -> dict:
    seeds = jax.random.split(jax.random.key(seed), 3)
    spectra = normal_values(seeds[0], (2, W, F, CHANNELS), 1.0, 6.0, ((2, 4), (3, 8)), jnp.float32)
    taps = normal_values(seeds[1], (F, TAPS), 0.25, 2.5, (), jnp.float32)
    return {"spectra": spectra, "taps": taps}


water_level = 0.1

def fan_filter(extended, coeffs, width):
    result = jnp.zeros(extended.shape[:-1] + (width,), jnp.float32)
    for tap_index in range(coeffs.shape[1]):
        result = result + coeffs[:, tap_index][:, None] * extended[..., tap_index:tap_index + width]
    return result

def whiten(filtered, amp_ext, local_bins):
    smoothed = jnp.zeros(filtered.shape[1:], jnp.float32)
    for offset in range(SMOOTH):
        smoothed = smoothed + amp_ext[:, offset:offset + local_bins, :]
    smoothed = smoothed / SMOOTH
    return (filtered / (smoothed + water_level)[None]).astype(jnp.bfloat16)

def arrange(whitened, band_count):
    shaped = whitened.reshape(2, whitened.shape[1], band_count, BAND_BINS, whitened.shape[3])
    shaped = shaped.transpose(2, 0, 1, 3, 4)
    return shaped.reshape(band_count, 2 * whitened.shape[1] * BAND_BINS, whitened.shape[3])

def partner(whitened):
    return jnp.concatenate([-whitened[1:2], whitened[0:1]], axis=0)

def reference(spectra, taps):
    half_taps = TAPS // 2
    extended = jnp.concatenate([spectra[..., CHANNELS - half_taps:], spectra, spectra[..., :half_taps]], axis=3)
    filtered = fan_filter(extended, taps, CHANNELS)
    amplitude = jnp.sqrt(filtered[0] * filtered[0] + filtered[1] * filtered[1])
    reach = SMOOTH // 2
    padded = jnp.pad(amplitude, ((0, 0), (reach, reach), (0, 0)))
    whitened = whiten(filtered, padded, F)
    features = arrange(whitened, BANDS)
    rotated = arrange(partner(whitened), BANDS)
    scale_factor = 1.0 / (W * BAND_BINS)
    dims = (((0,), (0,)), ((), ()))

    def one_band(index):
        left = features[index]
        real_part = lax.dot_general(left, left, dims, preferred_element_type=jnp.float32)
        imag_part = lax.dot_general(left, rotated[index], dims, preferred_element_type=jnp.float32)
        return (jnp.stack([real_part, imag_part]) * scale_factor).astype(jnp.bfloat16)
    return lax.map(one_band, jnp.arange(BANDS))
```

```python
from functools import partial

import jax
import jax.numpy as jnp
from jax import lax
from jax.experimental import pallas as pl
from jax.experimental.pallas import tpu as pltpu
from jax.sharding import PartitionSpec as P

SMOOTH = 5
BAND_BINS = 12
WATER = 0.1
MESH = pl.DeviceIdType.MESH
F32, BF16 = jnp.float32, jnp.bfloat16


def rolled(value, by, axis):
    if isinstance(by, int):
        by = by % value.shape[axis]
        if by == 0:
            return value
    return pltpu.roll(value, by, axis)


def kernel(
    n, m, x_ref, taps_ref, out_ref, coef, edge_out, edge_in, filt, amp, rim_out, rim_in, held, left,
    edge_send, edge_recv, rim_send, rim_recv, block_send, block_recv,
):
    windows, bins, lanes = x_ref.shape[1:]
    tap_count = taps_ref.shape[1]
    half = tap_count // 2
    per = lanes // half
    groups = windows // 4
    depth = held.shape[2]
    piece = depth // 2
    part = piece // 2
    me = lax.axis_index("chan")
    group = lax.axis_index("band")
    chan_up, chan_down = lax.rem(me + 1, n), lax.rem(me + n - 1, n)
    band_up, band_down = lax.rem(group + 1, m), lax.rem(group + m - 1, m)
    odd = lax.rem(me, 2)
    pos = (1 - odd) * lax.div(me, 2) + odd * (n - 1 - lax.div(me, 2))

    def place(p):
        far = lax.div(p, (n + 1) // 2)
        return (1 - far) * 2 * p + far * (2 * (n - 1 - p) + 1)

    ring = (place(lax.rem(pos + 1, n)), place(lax.rem(pos + n - 1, n)))

    barrier = pltpu.get_barrier_semaphore()
    for other in (chan_up, chan_down) + ring:
        pl.semaphore_signal(barrier, inc=1, device_id={"chan": other}, device_id_type=MESH)
    for other in (band_up, band_down):
        pl.semaphore_signal(barrier, inc=1, device_id={"band": other}, device_id_type=MESH)

    lane = lax.broadcasted_iota(jnp.int32, (bins, lanes), 1)
    for k in range(2):
        for e in range(windows // per):
            last = first = jnp.zeros((bins, lanes), F32)
            for q in range(per):
                v = x_ref[k, e * per + q]
                here = (lane >= half * q) & (lane < half * (q + 1))
                last = jnp.where(here, rolled(v, half * (q + 1), 1), last)
                first = jnp.where(here, rolled(v, half * q, 1), first)
            edge_out[0, k, e] = last
            edge_out[1, k, e] = first
    pl.semaphore_wait(barrier, 6)

    edges = [
        pltpu.make_async_remote_copy(
            src_ref=edge_out.at[i], dst_ref=edge_in.at[i], send_sem=edge_send.at[i],
            recv_sem=edge_recv.at[i], device_id={"chan": other}, device_id_type=MESH,
        )
        for i, other in enumerate((chan_up, chan_down))
    ]
    for copy in edges:
        copy.start()

    mine = taps_ref[pl.ds(pl.multiple_of(group * bins, 8), bins), :]
    for t in range(tap_count):
        coef[t] = jnp.broadcast_to(mine[:, t : t + 1], (bins, lanes))
    for copy in edges:
        copy.wait_recv()

    sub = lax.broadcasted_iota(jnp.int32, (8, lanes), 0)

    def filter_group(g, carry):
        e = lax.div(g, per // 4)
        top = bottom = jnp.zeros((8, lanes), F32)
        for u in range(4):
            w = 4 * g + u
            start = half * (4 * lax.rem(g, per // 4) + u)
            done = []
            for k in range(2):
                v = x_ref[k, w]
                h = jnp.where(
                    lane < half,
                    pltpu.roll(edge_in[1, k, e], lax.rem(lanes - start, lanes), 1),
                    pltpu.roll(edge_in[0, k, e], lanes - half - start, 1),
                )
                total = jnp.zeros((bins, lanes), F32)
                for t in range(tap_count):
                    s = t - half
                    if s < 0:
                        src = jnp.where(lane >= lanes + s, h, v)
                    elif s > 0:
                        src = jnp.where(lane < s, h, v)
                    else:
                        src = v
                    total = total + coef[t] * rolled(src, -s, 1)
                filt[k, w] = total
                done.append(total)
            a = jnp.sqrt(done[0] * done[0] + done[1] * done[1])
            amp[w, 8 : 8 + bins] = a
            here = (sub >= 2 * u) & (sub < 2 * u + 2)
            top = jnp.where(here, rolled(a[bins - 8 :], 2 * u - 6, 0), top)
            bottom = jnp.where(here, rolled(a[:8], 2 * u, 0), bottom)
        rim_out[0, g] = top
        rim_out[1, g] = bottom
        return carry

    lax.fori_loop(0, groups, filter_group, 0)

    rims = [
        pltpu.make_async_remote_copy(
            src_ref=rim_out.at[i], dst_ref=rim_in.at[i], send_sem=rim_send.at[i],
            recv_sem=rim_recv.at[i], device_id={"band": other}, device_id_type=MESH,
        )
        for i, other in enumerate((band_up, band_down))
    ]
    for copy in rims:
        copy.start()
    for copy in rims:
        copy.wait_recv()

    keep_before = jnp.where(group == 0, 0.0, 1.0).astype(F32)
    keep_after = jnp.where(group == m - 1, 0.0, 1.0).astype(F32)

    def whiten_group(g, carry):
        before, after = rim_in[0, g] * keep_before, rim_in[1, g] * keep_after
        shown = ([], [])
        for u in range(4):
            w = 4 * g + u
            amp[w, 0:8] = rolled(before, 6 - 2 * u, 0)
            amp[w, 8 + bins : 16 + bins] = rolled(after, -2 * u, 0)
            total = jnp.zeros((bins, lanes), F32)
            for d in range(SMOOTH):
                total = total + amp[w, 6 + d : 6 + d + bins]
            inverse = 1.0 / (total * (1.0 / SMOOTH) + WATER)
            for k in range(2):
                shown[k].append(filt[k, w] * inverse)
        for k in range(2):
            low, mid, high = ([v[8 * i : 8 * i + 8] for v in shown[k]] for i in range(3))
            mixed = ([], [])
            for u in (0, 2):
                mixed[0].append(jnp.where(sub < 4, mid[u], rolled(mid[u + 1], 4, 0)))
                mixed[1].append(jnp.where(sub < 4, rolled(mid[u], 4, 0), mid[u + 1]))
            row = lax.div(g, groups // 2) * piece + k * part + lax.rem(g, groups // 2) * 48
            rows = pl.ds(pl.multiple_of(row, 16), 48)
            held[0, 0, rows, :] = jnp.concatenate(low + mixed[0], axis=0).astype(BF16)
            held[0, 1, rows, :] = jnp.concatenate(high + mixed[1], axis=0).astype(BF16)
        return carry

    def block(d, p, s):
        rows = pl.ds(p * piece, piece)
        return pltpu.make_async_remote_copy(
            src_ref=held.at[s, d, rows], dst_ref=held.at[s + 1, d, rows],
            send_sem=block_send.at[d, p, s], recv_sem=block_recv.at[d, p, s + 1],
            device_id={"chan": ring[d]}, device_id_type=MESH,
        )

    for p in range(2):
        lax.fori_loop(p * groups // 2, (p + 1) * groups // 2, whiten_group, 0)
        for d in range(2):
            block(d, p, 0).start()

    for b in range(2):
        own = held[0, b].astype(F32)
        turned = []
        for p in range(2):
            turned.append(own[p * piece + part : (p + 1) * piece])
            turned.append(-own[p * piece : p * piece + part])
        left[b, 0:lanes] = own.T.astype(BF16)
        left[b, lanes : 2 * lanes] = jnp.concatenate(turned, axis=0).T.astype(BF16)

    scale = 1.0 / (windows * BAND_BINS)

    def cross(s):
        for d in range(2):
            owner = place(lax.rem(pos + n - s if d == 0 else pos + s, n))
            columns = pl.ds(pl.multiple_of(owner * lanes, lanes), lanes)
            tile = jnp.dot(left[d], held[s, d], preferred_element_type=F32)
            tile = (tile * scale).astype(BF16)
            out_ref[d, 0, :, columns] = tile[:lanes]
            out_ref[d, 1, :, columns] = tile[lanes:]

    cross(0)

    def step(s, carry):
        for p in range(2):
            for d in range(2):
                block(d, p, s - 1).wait_recv()
                block(d, p, s).start()
        cross(s)
        return carry

    lax.fori_loop(1, n - 1, step, 0)
    for p in range(2):
        for d in range(2):
            block(d, p, n - 2).wait_recv()
    cross(n - 1)

    def drain(s, carry):
        for p in range(2):
            for d in range(2):
                block(d, p, s).wait_send()
        return carry

    lax.fori_loop(0, n - 1, drain, 0)
    for copy in edges + rims:
        copy.wait_send()


def body(n, m, spectra, taps):
    _, windows, bins, lanes = spectra.shape
    half = taps.shape[1] // 2
    per = lanes // half
    bands = bins // BAND_BINS
    depth = 2 * windows * BAND_BINS
    vmem = pl.BlockSpec(memory_space=pltpu.VMEM)
    dma = pltpu.SemaphoreType.DMA
    return pl.pallas_call(
        partial(kernel, n, m),
        out_shape=jax.ShapeDtypeStruct((bands, 2, lanes, n * lanes), BF16),
        in_specs=[vmem] * 2,
        out_specs=vmem,
        scratch_shapes=[
            pltpu.VMEM((taps.shape[1], bins, lanes), F32),
            pltpu.VMEM((2, 2, windows // per, bins, lanes), F32),
            pltpu.VMEM((2, 2, windows // per, bins, lanes), F32),
            pltpu.VMEM((2, windows, bins, lanes), F32),
            pltpu.VMEM((windows, bins + 16, lanes), F32),
            pltpu.VMEM((2, windows // 4, 8, lanes), F32),
            pltpu.VMEM((2, windows // 4, 8, lanes), F32),
            pltpu.VMEM((n, bands, depth, lanes), BF16),
            pltpu.VMEM((bands, 2 * lanes, depth), BF16),
            dma((2,)),
            dma((2,)),
            dma((2,)),
            dma((2,)),
            dma((2, 2, n)),
            dma((2, 2, n)),
        ],
        compiler_params=pltpu.CompilerParams(
            collective_id=0, has_side_effects=True, vmem_limit_bytes=56 * 2**20
        ),
    )(spectra, taps)


def solution(mesh):
    placed = (P(None, None, "band", "chan"), P())
    return jax.shard_map(
        partial(body, mesh.shape["chan"], mesh.shape["band"]),
        mesh=mesh, in_specs=placed, out_specs=P("band", None, "chan", None), check_vma=False,
    )
```

```python
from functools import partial

import jax
import jax.numpy as jnp
from jax import lax
from jax.experimental import pallas as pl
from jax.experimental.pallas import tpu as pltpu
from jax.sharding import PartitionSpec as P

SMOOTH = 5
BAND_BINS = 12
WATER = 0.1
RETURNED = 3
PIECES = 4
MESH = pl.DeviceIdType.MESH
F32, BF16 = jnp.float32, jnp.bfloat16


def rolled(value, by, axis):
    if isinstance(by, int):
        by = by % value.shape[axis]
        if by == 0:
            return value
    return pltpu.roll(value, by, axis)


def kernel(
    n, m, bins, x_ref, taps_ref, out_ref, coef, taps_wide, turned_x, filt, amp, rim_out, rim_in, held, left,
    back_out, back_in, edge_send, edge_recv, rim_send, rim_recv, block_send, block_recv, back_send, back_recv,
):
    rows, lanes = x_ref.shape[1:]
    windows = rows // bins
    tap_count = taps_ref.shape[1]
    half = tap_count // 2
    groups = windows // 4
    depth = held.shape[2]
    piece = depth // PIECES
    part = piece // 2
    returned = back_in.shape[1]
    last = n - 1 - returned
    me = lax.axis_index("chan")
    group = lax.axis_index("band")
    chan_up, chan_down = lax.rem(me + 1, n), lax.rem(me + n - 1, n)
    band_up, band_down = lax.rem(group + 1, m), lax.rem(group + m - 1, m)
    odd = lax.rem(me, 2)
    pos = (1 - odd) * lax.div(me, 2) + odd * (n - 1 - lax.div(me, 2))

    def place(p):
        far = lax.div(p, (n + 1) // 2)
        return (1 - far) * 2 * p + far * (2 * (n - 1 - p) + 1)

    def at(d, s):
        return place(lax.rem(pos + s if d == 0 else pos + n - s, n))

    ring = (at(0, 1), at(1, 1))
    reached = [at(d, s) for s in range(1, max(1, returned) + 1) for d in range(2)]

    barrier = pltpu.get_barrier_semaphore()
    for other in [chan_up, chan_down] + reached:
        pl.semaphore_signal(barrier, inc=1, device_id={"chan": other}, device_id_type=MESH)
    for other in (band_up, band_down):
        pl.semaphore_signal(barrier, inc=1, device_id={"band": other}, device_id_type=MESH)

    for k in range(2):
        for j in range(0, rows, lanes):
            turned_x[k, half : half + lanes, j : j + lanes] = x_ref[k, j : j + lanes].T
    pl.semaphore_wait(barrier, len(reached) + 4)

    edges = [
        pltpu.make_async_remote_copy(
            src_ref=turned_x.at[:, pl.ds(src, half)], dst_ref=turned_x.at[:, pl.ds(dst, half)],
            send_sem=edge_send.at[i], recv_sem=edge_recv.at[i],
            device_id={"chan": other}, device_id_type=MESH,
        )
        for i, (other, src, dst) in enumerate(
            ((chan_up, lanes, 0), (chan_down, half, half + lanes))
        )
    ]
    for copy in edges:
        copy.start()

    mine = taps_ref[pl.ds(pl.multiple_of(group * bins, 8), bins), :]
    taps_wide[...] = jnp.zeros(taps_wide.shape, F32)
    taps_wide[:, 0:tap_count] = mine
    wide = taps_wide[...]
    coef[...] = jnp.concatenate([wide] * (windows // 2), axis=0).T[:tap_count]
    for copy in edges:
        copy.wait_recv()

    sub = lax.broadcasted_iota(jnp.int32, (8, lanes), 0)

    def filter_half(h):
        def tile(j, carry):
            here = pl.ds(pl.multiple_of(j * lanes, lanes), lanes)
            cols = pl.ds(pl.multiple_of(h * (rows // 2) + j * lanes, lanes), lanes)
            for k in range(2):
                done = []
                for r in range(0, lanes, lanes // 2):
                    total = jnp.zeros((lanes // 2, lanes), F32)
                    for t in range(tap_count):
                        total = total + coef[t : t + 1, here] * turned_x[k, r + t : r + t + lanes // 2, cols]
                    done.append(total)
                filt[k, cols, :] = jnp.concatenate(done, axis=0).T
            return carry

        lax.fori_loop(0, rows // 2 // lanes, tile, 0)

    def bins_of(w):
        return pl.ds(pl.multiple_of(w * bins, 8), bins)

    def amplitude_group(g, carry):
        top = bottom = jnp.zeros((8, lanes), F32)
        for u in range(4):
            w = 4 * g + u
            re, im = filt[0, bins_of(w), :], filt[1, bins_of(w), :]
            a = jnp.sqrt(re * re + im * im)
            amp[w, 8 : 8 + bins] = a
            here = (sub >= 2 * u) & (sub < 2 * u + 2)
            top = jnp.where(here, rolled(a[bins - 8 :], 2 * u - 6, 0), top)
            bottom = jnp.where(here, rolled(a[:8], 2 * u, 0), bottom)
        rim_out[0, g] = top
        rim_out[1, g] = bottom
        return carry

    rims = []
    for h in range(2):
        filter_half(h)
        lax.fori_loop(h * groups // 2, (h + 1) * groups // 2, amplitude_group, 0)
        some = pl.ds(h * groups // 2, groups // 2)
        rims.append(
            [
                pltpu.make_async_remote_copy(
                    src_ref=rim_out.at[i, some], dst_ref=rim_in.at[i, some],
                    send_sem=rim_send.at[i, h], recv_sem=rim_recv.at[i, h],
                    device_id={"band": other}, device_id_type=MESH,
                )
                for i, other in enumerate((band_up, band_down))
            ]
        )
        for copy in rims[h]:
            copy.start()

    keep_before = jnp.where(group == 0, 0.0, 1.0).astype(F32)
    keep_after = jnp.where(group == m - 1, 0.0, 1.0).astype(F32)

    def whiten_group(g, carry):
        before, after = rim_in[0, g] * keep_before, rim_in[1, g] * keep_after
        shown = ([], [])
        for u in range(4):
            w = 4 * g + u
            amp[w, 0:8] = rolled(before, 6 - 2 * u, 0)
            amp[w, 8 + bins : 16 + bins] = rolled(after, -2 * u, 0)
            total = jnp.zeros((bins, lanes), F32)
            for d in range(SMOOTH):
                total = total + amp[w, 6 + d : 6 + d + bins]
            inverse = 1.0 / (total * (1.0 / SMOOTH) + WATER)
            for k in range(2):
                shown[k].append(filt[k, bins_of(w), :] * inverse)
        for k in range(2):
            low, mid, high = ([v[8 * i : 8 * i + 8] for v in shown[k]] for i in range(3))
            mixed = ([], [])
            for u in (0, 2):
                mixed[0].append(jnp.where(sub < 4, mid[u], rolled(mid[u + 1], 4, 0)))
                mixed[1].append(jnp.where(sub < 4, rolled(mid[u], 4, 0), mid[u + 1]))
            row = lax.div(g, groups // PIECES) * piece + k * part + lax.rem(g, groups // PIECES) * 48
            chunk = pl.ds(pl.multiple_of(row, 16), 48)
            held[0, 0, chunk, :] = jnp.concatenate(low + mixed[0], axis=0).astype(BF16)
            held[0, 1, chunk, :] = jnp.concatenate(high + mixed[1], axis=0).astype(BF16)
        return carry

    def block(d, p, s):
        chunk = pl.ds(p * piece, piece)
        return pltpu.make_async_remote_copy(
            src_ref=held.at[s, d, chunk], dst_ref=held.at[s + 1, d, chunk],
            send_sem=block_send.at[d, p, s], recv_sem=block_recv.at[d, p, s + 1],
            device_id={"chan": ring[d]}, device_id_type=MESH,
        )

    for p in range(PIECES):
        if p % (PIECES // 2) == 0:
            for copy in rims[p // (PIECES // 2)]:
                copy.wait_recv()
        lax.fori_loop(p * groups // PIECES, (p + 1) * groups // PIECES, whiten_group, 0)
        for d in range(2):
            block(d, p, 0).start()

    for b in range(2):
        own = held[0, b].astype(F32)
        turned = []
        for p in range(PIECES):
            turned.append(own[p * piece + part : (p + 1) * piece])
            turned.append(-own[p * piece : p * piece + part])
        left[b, 0:lanes] = own.T.astype(BF16)
        left[b, lanes : 2 * lanes] = jnp.concatenate(turned, axis=0).T.astype(BF16)

    scale = 1.0 / (windows * BAND_BINS)

    def back(d, s):
        return pltpu.make_async_remote_copy(
            src_ref=back_out.at[d, s - 1], dst_ref=back_in.at[d, s - 1],
            send_sem=back_send.at[d, s - 1], recv_sem=back_recv.at[d, s - 1],
            device_id={"chan": at(1 - d, s)}, device_id_type=MESH,
        )

    def columns(owner):
        return pl.ds(pl.multiple_of(owner * lanes, lanes), lanes)

    def cross(s, send_back=False):
        for d in range(2):
            tile = jnp.dot(left[d], held[s, d], preferred_element_type=F32) * scale
            if send_back:
                back_out[d, s - 1, 0] = tile[:lanes].T.astype(BF16)
                back_out[d, s - 1, 1] = (-tile[lanes:]).T.astype(BF16)
                back(d, s).start()
            tile = tile.astype(BF16)
            here = columns(at(1 - d, s))
            out_ref[d, 0, :, here] = tile[:lanes]
            out_ref[d, 1, :, here] = tile[lanes:]

    cross(0)

    def step(s, carry, send_back=False):
        for p in range(PIECES):
            for d in range(2):
                block(d, p, s - 1).wait_recv()
                block(d, p, s).start()
        cross(s, send_back)
        return carry

    for s in range(1, returned + 1):
        step(s, 0, True)
    lax.fori_loop(returned + 1, last, step, 0)
    for p in range(PIECES):
        for d in range(2):
            block(d, p, last - 1).wait_recv()
    cross(last)
    for s in range(1, returned + 1):
        for d in range(2):
            back(d, s).wait_recv()
            here = columns(at(d, s))
            out_ref[d, 0, :, here] = back_in[d, s - 1, 0]
            out_ref[d, 1, :, here] = back_in[d, s - 1, 1]

    def drain(s, carry):
        for p in range(PIECES):
            for d in range(2):
                block(d, p, s).wait_send()
        return carry

    lax.fori_loop(0, last, drain, 0)
    for s in range(1, returned + 1):
        for d in range(2):
            back(d, s).wait_send()
    for copy in edges + rims[0] + rims[1]:
        copy.wait_send()


def body(n, m, spectra, taps):
    _, windows, bins, lanes = spectra.shape
    taps_count = taps.shape[1]
    returned = min(RETURNED, (n - 2) // 2)
    bands = bins // BAND_BINS
    depth = 2 * windows * BAND_BINS
    vmem = pl.BlockSpec(memory_space=pltpu.VMEM)
    dma = pltpu.SemaphoreType.DMA
    return pl.pallas_call(
        partial(kernel, n, m, bins),
        out_shape=jax.ShapeDtypeStruct((bands, 2, lanes, n * lanes), BF16),
        in_specs=[vmem] * 2,
        out_specs=vmem,
        scratch_shapes=[
            pltpu.VMEM((taps_count, windows * bins // 2), F32),
            pltpu.VMEM((bins, lanes), F32),
            pltpu.VMEM((2, lanes + taps_count, windows * bins), F32),
            pltpu.VMEM((2, windows * bins, lanes), F32),
            pltpu.VMEM((windows, bins + 16, lanes), F32),
            pltpu.VMEM((2, windows // 4, 8, lanes), F32),
            pltpu.VMEM((2, windows // 4, 8, lanes), F32),
            pltpu.VMEM((n - returned, bands, depth, lanes), BF16),
            pltpu.VMEM((bands, 2 * lanes, depth), BF16),
            pltpu.VMEM((2, returned, 2, lanes, lanes), BF16),
            pltpu.VMEM((2, returned, 2, lanes, lanes), BF16),
            dma((2,)),
            dma((2,)),
            dma((2, 2)),
            dma((2, 2)),
            dma((2, PIECES, n)),
            dma((2, PIECES, n)),
            dma((2, returned)),
            dma((2, returned)),
        ],
        compiler_params=pltpu.CompilerParams(
            collective_id=0, has_side_effects=True, vmem_limit_bytes=56 * 2**20
        ),
    )(spectra.reshape(2, windows * bins, lanes), taps)


def solution(mesh):
    placed = (P(None, None, "band", "chan"), P())
    return jax.shard_map(
        partial(body, mesh.shape["chan"], mesh.shape["band"]),
        mesh=mesh, in_specs=placed, out_specs=P("band", None, "chan", None), check_vma=False,
    )
```

```python
from functools import partial

import jax
import jax.numpy as jnp
from jax import lax
from jax.experimental import pallas as pl
from jax.experimental.pallas import tpu as pltpu
from jax.sharding import PartitionSpec as P

SMOOTH = 5
BAND_BINS = 12
WATER = 0.1
RETURNED = 3
PIECES = 4
MESH = pl.DeviceIdType.MESH
F32, BF16 = jnp.float32, jnp.bfloat16


def rolled(value, by, axis):
    if isinstance(by, int):
        by = by % value.shape[axis]
        if by == 0:
            return value
    return pltpu.roll(value, by, axis)


def kernel(
    n, m, bins, x_hbm, taps_hbm, out_ref, x_ref, taps_ref, load_sem, coef, taps_wide, taps_turned, turned_x, mid, filt, amp, rim_out, rim_in, held, left,
    back_out, back_in, edge_send, edge_recv, rim_send, rim_recv, block_send, block_recv, back_send, back_recv,
):
    rows, lanes = x_ref.shape[1:]
    windows = rows // bins
    tap_count, all_bins = taps_ref.shape
    half = tap_count // 2
    groups = windows // 4
    depth = held.shape[2]
    piece = depth // PIECES
    part = piece // 2
    returned = back_in.shape[1]
    last = n - 1 - returned
    loads = [
        pltpu.make_async_copy(x_hbm.at[k], x_ref.at[k], load_sem.at[k]) for k in range(2)
    ] + [pltpu.make_async_copy(taps_hbm, taps_ref, load_sem.at[2])]
    for load in loads:
        load.start()
    me = lax.axis_index("chan")
    group = lax.axis_index("band")
    chan_up, chan_down = lax.rem(me + 1, n), lax.rem(me + n - 1, n)
    band_up, band_down = lax.rem(group + 1, m), lax.rem(group + m - 1, m)
    odd = lax.rem(me, 2)
    pos = (1 - odd) * lax.div(me, 2) + odd * (n - 1 - lax.div(me, 2))

    def place(p):
        far = lax.div(p, (n + 1) // 2)
        return (1 - far) * 2 * p + far * (2 * (n - 1 - p) + 1)

    def at(d, s):
        return place(lax.rem(pos + s if d == 0 else pos + n - s, n))

    ring = (at(0, 1), at(1, 1))
    reached = [at(d, s) for s in range(1, max(1, returned) + 1) for d in range(2)]

    barrier = pltpu.get_barrier_semaphore()
    for other in [chan_up, chan_down] + reached:
        pl.semaphore_signal(barrier, inc=1, device_id={"chan": other}, device_id_type=MESH)
    for other in (band_up, band_down):
        pl.semaphore_signal(barrier, inc=1, device_id={"band": other}, device_id_type=MESH)

    for k in range(2):
        loads[k].wait()
        for j in range(0, rows, lanes):
            turned_x[k, half : half + lanes, j : j + lanes] = x_ref[k, j : j + lanes].T
    pl.semaphore_wait(barrier, len(reached) + 4)

    edges = [
        pltpu.make_async_remote_copy(
            src_ref=turned_x.at[:, pl.ds(src, half)], dst_ref=turned_x.at[:, pl.ds(dst, half)],
            send_sem=edge_send.at[i], recv_sem=edge_recv.at[i],
            device_id={"chan": other}, device_id_type=MESH,
        )
        for i, (other, src, dst) in enumerate(
            ((chan_up, lanes, 0), (chan_down, half, half + lanes))
        )
    ]
    for copy in edges:
        copy.start()

    loads[2].wait()
    taps_wide[...] = jnp.zeros(taps_wide.shape, F32)
    taps_wide[0:tap_count, 0:all_bins] = taps_ref[...]
    taps_turned[...] = taps_wide[...].T
    wide = taps_turned[pl.ds(pl.multiple_of(group * bins, 8), bins), :]
    coef[...] = jnp.concatenate([wide] * (windows // 2), axis=0).T[:tap_count]
    def summed(k, start, count, here, cols):
        total = jnp.zeros((count, lanes), F32)
        for t in range(tap_count):
            total = total + coef[t : t + 1, here] * turned_x[k, start + t : start + t + count, cols]
        return total

    def tile_of(j):
        here = lax.rem(j, rows // 2 // lanes) * lanes
        return pl.ds(pl.multiple_of(here, lanes), lanes), pl.ds(pl.multiple_of(j * lanes, lanes), lanes)

    inner = lanes // 2 - half

    def inner_tile(j, carry):
        here, cols = tile_of(j)
        for k in range(2):
            for start in (half, half + inner):
                mid[k, start : start + inner, cols] = summed(k, start, inner, here, cols)
        return carry

    lax.fori_loop(0, rows // lanes, inner_tile, 0)
    for copy in edges:
        copy.wait_recv()

    sub = lax.broadcasted_iota(jnp.int32, (8, lanes), 0)

    def filter_half(h):
        def tile(j, carry):
            here, cols = tile_of(j)
            for k in range(2):
                parts = [
                    summed(k, 0, half, here, cols),
                    mid[k, half : lanes - half, cols],
                    summed(k, lanes - half, half, here, cols),
                ]
                filt[k, cols, :] = jnp.concatenate(parts, axis=0).T
            return carry

        tiles = rows // lanes
        lax.fori_loop(h * tiles // 2, (h + 1) * tiles // 2, tile, 0)

    def bins_of(w):
        return pl.ds(pl.multiple_of(w * bins, 8), bins)

    def amplitude_group(g, carry):
        top = bottom = jnp.zeros((8, lanes), F32)
        for u in range(4):
            w = 4 * g + u
            re, im = filt[0, bins_of(w), :], filt[1, bins_of(w), :]
            a = jnp.sqrt(re * re + im * im)
            amp[w, 8 : 8 + bins] = a
            here = (sub >= 2 * u) & (sub < 2 * u + 2)
            top = jnp.where(here, rolled(a[bins - 8 :], 2 * u - 6, 0), top)
            bottom = jnp.where(here, rolled(a[:8], 2 * u, 0), bottom)
        rim_out[0, g] = top
        rim_out[1, g] = bottom
        return carry

    rims = []
    for h in range(2):
        filter_half(h)
        lax.fori_loop(h * groups // 2, (h + 1) * groups // 2, amplitude_group, 0)
        some = pl.ds(h * groups // 2, groups // 2)
        rims.append(
            [
                pltpu.make_async_remote_copy(
                    src_ref=rim_out.at[i, some], dst_ref=rim_in.at[i, some],
                    send_sem=rim_send.at[i, h], recv_sem=rim_recv.at[i, h],
                    device_id={"band": other}, device_id_type=MESH,
                )
                for i, other in enumerate((band_up, band_down))
            ]
        )
        for copy in rims[h]:
            copy.start()

    keep_before = jnp.where(group == 0, 0.0, 1.0).astype(F32)
    keep_after = jnp.where(group == m - 1, 0.0, 1.0).astype(F32)

    def whiten_group(g, carry):
        before, after = rim_in[0, g] * keep_before, rim_in[1, g] * keep_after
        shown = ([], [])
        for u in range(4):
            w = 4 * g + u
            amp[w, 0:8] = rolled(before, 6 - 2 * u, 0)
            amp[w, 8 + bins : 16 + bins] = rolled(after, -2 * u, 0)
            total = jnp.zeros((bins, lanes), F32)
            for d in range(SMOOTH):
                total = total + amp[w, 6 + d : 6 + d + bins]
            inverse = 1.0 / (total * (1.0 / SMOOTH) + WATER)
            for k in range(2):
                shown[k].append(filt[k, bins_of(w), :] * inverse)
        for k in range(2):
            low, mid, high = ([v[8 * i : 8 * i + 8] for v in shown[k]] for i in range(3))
            mixed = ([], [])
            for u in (0, 2):
                mixed[0].append(jnp.where(sub < 4, mid[u], rolled(mid[u + 1], 4, 0)))
                mixed[1].append(jnp.where(sub < 4, rolled(mid[u], 4, 0), mid[u + 1]))
            row = lax.div(g, groups // PIECES) * piece + k * part + lax.rem(g, groups // PIECES) * 48
            chunk = pl.ds(pl.multiple_of(row, 16), 48)
            held[0, 0, chunk, :] = jnp.concatenate(low + mixed[0], axis=0).astype(BF16)
            held[0, 1, chunk, :] = jnp.concatenate(high + mixed[1], axis=0).astype(BF16)
        return carry

    def block(d, p, s):
        chunk = pl.ds(p * piece, piece)
        return pltpu.make_async_remote_copy(
            src_ref=held.at[s, d, chunk], dst_ref=held.at[s + 1, d, chunk],
            send_sem=block_send.at[d, p, s], recv_sem=block_recv.at[d, p, s + 1],
            device_id={"chan": ring[d]}, device_id_type=MESH,
        )

    for p in range(PIECES):
        if p % (PIECES // 2) == 0:
            for copy in rims[p // (PIECES // 2)]:
                copy.wait_recv()
        lax.fori_loop(p * groups // PIECES, (p + 1) * groups // PIECES, whiten_group, 0)
        for d in range(2):
            block(d, p, 0).start()

    for b in range(2):
        own = held[0, b].astype(F32)
        turned = []
        for p in range(PIECES):
            turned.append(own[p * piece + part : (p + 1) * piece])
            turned.append(-own[p * piece : p * piece + part])
        left[b, 0:lanes] = own.T.astype(BF16)
        left[b, lanes : 2 * lanes] = jnp.concatenate(turned, axis=0).T.astype(BF16)

    scale = 1.0 / (windows * BAND_BINS)

    def back(d, s):
        return pltpu.make_async_remote_copy(
            src_ref=back_out.at[d, s - 1], dst_ref=back_in.at[d, s - 1],
            send_sem=back_send.at[d, s - 1], recv_sem=back_recv.at[d, s - 1],
            device_id={"chan": at(1 - d, s)}, device_id_type=MESH,
        )

    def columns(owner):
        return pl.ds(pl.multiple_of(owner * lanes, lanes), lanes)

    def cross(s, send_back=False):
        for d in range(2):
            tile = jnp.dot(left[d], held[s, d], preferred_element_type=F32) * scale
            if send_back:
                back_out[d, s - 1, 0] = tile[:lanes].T.astype(BF16)
                back_out[d, s - 1, 1] = (-tile[lanes:]).T.astype(BF16)
                back(d, s).start()
            tile = tile.astype(BF16)
            here = columns(at(1 - d, s))
            out_ref[d, 0, :, here] = tile[:lanes]
            out_ref[d, 1, :, here] = tile[lanes:]

    cross(0)

    def step(s, carry, send_back=False):
        for p in range(PIECES):
            for d in range(2):
                block(d, p, s - 1).wait_recv()
                block(d, p, s).start()
        cross(s, send_back)
        return carry

    for s in range(1, returned + 1):
        step(s, 0, True)
    lax.fori_loop(returned + 1, last, step, 0)
    for p in range(PIECES):
        for d in range(2):
            block(d, p, last - 1).wait_recv()
    cross(last)
    for s in range(1, returned + 1):
        for d in range(2):
            back(d, s).wait_recv()
            here = columns(at(d, s))
            out_ref[d, 0, :, here] = back_in[d, s - 1, 0]
            out_ref[d, 1, :, here] = back_in[d, s - 1, 1]

    def drain(s, carry):
        for p in range(PIECES):
            for d in range(2):
                block(d, p, s).wait_send()
        return carry

    lax.fori_loop(0, last, drain, 0)
    for s in range(1, returned + 1):
        for d in range(2):
            back(d, s).wait_send()
    for copy in edges + rims[0] + rims[1]:
        copy.wait_send()


def body(n, m, spectra, taps):
    _, windows, bins, lanes = spectra.shape
    taps_count = taps.shape[1]
    returned = min(RETURNED, (n - 2) // 2)
    wide = pl.cdiv(taps.shape[0], lanes) * lanes
    bands = bins // BAND_BINS
    depth = 2 * windows * BAND_BINS
    vmem = pl.BlockSpec(memory_space=pltpu.VMEM)
    dma = pltpu.SemaphoreType.DMA
    return pl.pallas_call(
        partial(kernel, n, m, bins),
        out_shape=jax.ShapeDtypeStruct((bands, 2, lanes, n * lanes), BF16),
        in_specs=[pl.BlockSpec(memory_space=pltpu.HBM)] * 2,
        out_specs=vmem,
        scratch_shapes=[
            pltpu.VMEM((2, windows * bins, lanes), F32),
            pltpu.VMEM(taps.shape[::-1], F32),
            dma((3,)),
            pltpu.VMEM((taps_count, windows * bins // 2), F32),
            pltpu.VMEM((lanes, wide), F32),
            pltpu.VMEM((wide, lanes), F32),
            pltpu.VMEM((2, lanes + taps_count, windows * bins), F32),
            pltpu.VMEM((2, lanes, windows * bins), F32),
            pltpu.VMEM((2, windows * bins, lanes), F32),
            pltpu.VMEM((windows, bins + 16, lanes), F32),
            pltpu.VMEM((2, windows // 4, 8, lanes), F32),
            pltpu.VMEM((2, windows // 4, 8, lanes), F32),
            pltpu.VMEM((n - returned, bands, depth, lanes), BF16),
            pltpu.VMEM((bands, 2 * lanes, depth), BF16),
            pltpu.VMEM((2, returned, 2, lanes, lanes), BF16),
            pltpu.VMEM((2, returned, 2, lanes, lanes), BF16),
            dma((2,)),
            dma((2,)),
            dma((2, 2)),
            dma((2, 2)),
            dma((2, PIECES, n)),
            dma((2, PIECES, n)),
            dma((2, returned)),
            dma((2, returned)),
        ],
        compiler_params=pltpu.CompilerParams(
            collective_id=0, has_side_effects=True, vmem_limit_bytes=56 * 2**20
        ),
    )(spectra.reshape(2, windows * bins, lanes), taps.T)


def solution(mesh):
    placed = (P(None, None, "band", "chan"), P())
    return jax.shard_map(
        partial(body, mesh.shape["chan"], mesh.shape["band"]),
        mesh=mesh, in_specs=placed, out_specs=P("band", None, "chan", None), check_vma=False,
    )
```

```python
from functools import partial

import jax
import jax.numpy as jnp
from jax import lax
from jax.experimental import pallas as pl
from jax.experimental.pallas import tpu as pltpu
from jax.sharding import PartitionSpec as P

SMOOTH = 5
BAND_BINS = 12
WATER = 0.1
RETURNED = 3
PIECES = 4
MESH = pl.DeviceIdType.MESH
F32, BF16 = jnp.float32, jnp.bfloat16


def rolled(value, by, axis):
    if isinstance(by, int):
        by = by % value.shape[axis]
        if by == 0:
            return value
    return pltpu.roll(value, by, axis)


def kernel(
    n, m, bins, x_hbm, taps_hbm, out_ref, x_ref, taps_ref, load_sem, coef, taps_wide, taps_turned, turned_x, mid, filt, amp, rim_out, rim_in, held, left,
    back_out, back_in, edge_send, edge_recv, rim_send, rim_recv, block_send, block_recv, back_send, back_recv,
):
    rows, lanes = x_ref.shape[1:]
    windows = rows // bins
    tap_count, all_bins = taps_ref.shape
    half = tap_count // 2
    groups = windows // 4
    depth = held.shape[2]
    piece = depth // PIECES
    part = piece // 2
    returned = back_in.shape[1]
    last = n - 1 - returned
    loads = [
        pltpu.make_async_copy(x_hbm.at[k], x_ref.at[k], load_sem.at[k]) for k in range(2)
    ] + [pltpu.make_async_copy(taps_hbm, taps_ref, load_sem.at[2])]
    for load in loads:
        load.start()
    me = lax.axis_index("chan")
    group = lax.axis_index("band")
    chan_up, chan_down = lax.rem(me + 1, n), lax.rem(me + n - 1, n)
    band_up, band_down = lax.rem(group + 1, m), lax.rem(group + m - 1, m)
    odd = lax.rem(me, 2)
    pos = (1 - odd) * lax.div(me, 2) + odd * (n - 1 - lax.div(me, 2))

    def place(p):
        far = lax.div(p, (n + 1) // 2)
        return (1 - far) * 2 * p + far * (2 * (n - 1 - p) + 1)

    def at(d, s):
        return place(lax.rem(pos + s if d == 0 else pos + n - s, n))

    ring = (at(0, 1), at(1, 1))
    reached = [at(d, s) for s in range(1, max(1, returned) + 1) for d in range(2)]

    barrier = pltpu.get_barrier_semaphore()
    for other in [chan_up, chan_down] + reached:
        pl.semaphore_signal(barrier, inc=1, device_id={"chan": other}, device_id_type=MESH)
    for other in (band_up, band_down):
        pl.semaphore_signal(barrier, inc=1, device_id={"band": other}, device_id_type=MESH)

    for k in range(2):
        loads[k].wait()
        for j in range(0, rows, lanes):
            turned_x[k, half : half + lanes, j : j + lanes] = x_ref[k, j : j + lanes].T
    pl.semaphore_wait(barrier, len(reached) + 4)

    edges = [
        pltpu.make_async_remote_copy(
            src_ref=turned_x.at[:, pl.ds(src, half)], dst_ref=turned_x.at[:, pl.ds(dst, half)],
            send_sem=edge_send.at[i], recv_sem=edge_recv.at[i],
            device_id={"chan": other}, device_id_type=MESH,
        )
        for i, (other, src, dst) in enumerate(
            ((chan_up, lanes, 0), (chan_down, half, half + lanes))
        )
    ]
    for copy in edges:
        copy.start()

    loads[2].wait()
    taps_wide[...] = jnp.zeros(taps_wide.shape, F32)
    taps_wide[0:tap_count, 0:all_bins] = taps_ref[...]
    taps_turned[...] = taps_wide[...].T
    wide = taps_turned[pl.ds(pl.multiple_of(group * bins, 8), bins), :]
    coef[...] = jnp.concatenate([wide] * (windows // 2), axis=0).T[:tap_count]
    def summed(k, start, count, here, cols):
        total = jnp.zeros((count, lanes), F32)
        for t in range(tap_count):
            total = total + coef[t : t + 1, here] * turned_x[k, start + t : start + t + count, cols]
        return total

    def tile_of(j):
        here = lax.rem(j, rows // 2 // lanes) * lanes
        return pl.ds(pl.multiple_of(here, lanes), lanes), pl.ds(pl.multiple_of(j * lanes, lanes), lanes)

    inner = lanes // 2 - half

    def inner_tile(j, carry):
        here, cols = tile_of(j)
        for k in range(2):
            for start in (half, half + inner):
                mid[k, start : start + inner, cols] = summed(k, start, inner, here, cols)
        return carry

    lax.fori_loop(0, rows // lanes, inner_tile, 0, unroll=True)
    for copy in edges:
        copy.wait_recv()

    sub = lax.broadcasted_iota(jnp.int32, (8, lanes), 0)

    def filter_half(h):
        def tile(j, carry):
            here, cols = tile_of(j)
            for k in range(2):
                parts = [
                    summed(k, 0, half, here, cols),
                    mid[k, half : lanes - half, cols],
                    summed(k, lanes - half, half, here, cols),
                ]
                filt[k, cols, :] = jnp.concatenate(parts, axis=0).T
            return carry

        tiles = rows // lanes
        lax.fori_loop(h * tiles // 2, (h + 1) * tiles // 2, tile, 0, unroll=True)

    def bins_of(w):
        return pl.ds(pl.multiple_of(w * bins, 8), bins)

    def amplitude_group(g, carry):
        top = bottom = jnp.zeros((8, lanes), F32)
        for u in range(4):
            w = 4 * g + u
            re, im = filt[0, bins_of(w), :], filt[1, bins_of(w), :]
            a = jnp.sqrt(re * re + im * im)
            amp[w, 8 : 8 + bins] = a
            here = (sub >= 2 * u) & (sub < 2 * u + 2)
            top = jnp.where(here, rolled(a[bins - 8 :], 2 * u - 6, 0), top)
            bottom = jnp.where(here, rolled(a[:8], 2 * u, 0), bottom)
        rim_out[0, g] = top
        rim_out[1, g] = bottom
        return carry

    rims = []
    for h in range(2):
        filter_half(h)
        lax.fori_loop(h * groups // 2, (h + 1) * groups // 2, amplitude_group, 0, unroll=True)
        some = pl.ds(h * groups // 2, groups // 2)
        rims.append(
            [
                pltpu.make_async_remote_copy(
                    src_ref=rim_out.at[i, some], dst_ref=rim_in.at[i, some],
                    send_sem=rim_send.at[i, h], recv_sem=rim_recv.at[i, h],
                    device_id={"band": other}, device_id_type=MESH,
                )
                for i, other in enumerate((band_up, band_down))
            ]
        )
        for copy in rims[h]:
            copy.start()

    keep_before = jnp.where(group == 0, 0.0, 1.0).astype(F32)
    keep_after = jnp.where(group == m - 1, 0.0, 1.0).astype(F32)

    def whiten_group(g, carry):
        before, after = rim_in[0, g] * keep_before, rim_in[1, g] * keep_after
        shown = ([], [])
        for u in range(4):
            w = 4 * g + u
            amp[w, 0:8] = rolled(before, 6 - 2 * u, 0)
            amp[w, 8 + bins : 16 + bins] = rolled(after, -2 * u, 0)
            total = jnp.zeros((bins, lanes), F32)
            for d in range(SMOOTH):
                total = total + amp[w, 6 + d : 6 + d + bins]
            inverse = 1.0 / (total * (1.0 / SMOOTH) + WATER)
            for k in range(2):
                shown[k].append(filt[k, bins_of(w), :] * inverse)
        for k in range(2):
            low, mid, high = ([v[8 * i : 8 * i + 8] for v in shown[k]] for i in range(3))
            mixed = ([], [])
            for u in (0, 2):
                mixed[0].append(jnp.where(sub < 4, mid[u], rolled(mid[u + 1], 4, 0)))
                mixed[1].append(jnp.where(sub < 4, rolled(mid[u], 4, 0), mid[u + 1]))
            row = lax.div(g, groups // PIECES) * piece + k * part + lax.rem(g, groups // PIECES) * 48
            chunk = pl.ds(pl.multiple_of(row, 16), 48)
            held[0, 0, chunk, :] = jnp.concatenate(low + mixed[0], axis=0).astype(BF16)
            held[0, 1, chunk, :] = jnp.concatenate(high + mixed[1], axis=0).astype(BF16)
        return carry

    def block(d, p, s):
        chunk = pl.ds(p * piece, piece)
        return pltpu.make_async_remote_copy(
            src_ref=held.at[s, d, chunk], dst_ref=held.at[s + 1, d, chunk],
            send_sem=block_send.at[d, p, s], recv_sem=block_recv.at[d, p, s + 1],
            device_id={"chan": ring[d]}, device_id_type=MESH,
        )

    for p in range(PIECES):
        if p % (PIECES // 2) == 0:
            for copy in rims[p // (PIECES // 2)]:
                copy.wait_recv()
        lax.fori_loop(p * groups // PIECES, (p + 1) * groups // PIECES, whiten_group, 0, unroll=True)
        for d in range(2):
            block(d, p, 0).start()

    for b in range(2):
        own = held[0, b].astype(F32)
        turned = []
        for p in range(PIECES):
            turned.append(own[p * piece + part : (p + 1) * piece])
            turned.append(-own[p * piece : p * piece + part])
        left[b, 0:lanes] = own.T.astype(BF16)
        left[b, lanes : 2 * lanes] = jnp.concatenate(turned, axis=0).T.astype(BF16)

    scale = 1.0 / (windows * BAND_BINS)

    def back(d, s):
        return pltpu.make_async_remote_copy(
            src_ref=back_out.at[d, s - 1], dst_ref=back_in.at[d, s - 1],
            send_sem=back_send.at[d, s - 1], recv_sem=back_recv.at[d, s - 1],
            device_id={"chan": at(1 - d, s)}, device_id_type=MESH,
        )

    def columns(owner):
        return pl.ds(pl.multiple_of(owner * lanes, lanes), lanes)

    def cross(s, send_back=False):
        for d in range(2):
            tile = jnp.dot(left[d], held[s, d], preferred_element_type=F32) * scale
            if send_back:
                back_out[d, s - 1, 0] = tile[:lanes].T.astype(BF16)
                back_out[d, s - 1, 1] = (-tile[lanes:]).T.astype(BF16)
                back(d, s).start()
            tile = tile.astype(BF16)
            here = columns(at(1 - d, s))
            out_ref[d, 0, :, here] = tile[:lanes]
            out_ref[d, 1, :, here] = tile[lanes:]

    cross(0)

    def step(s, carry, send_back=False):
        for p in range(PIECES):
            for d in range(2):
                block(d, p, s - 1).wait_recv()
                block(d, p, s).start()
        cross(s, send_back)
        return carry

    for s in range(1, returned + 1):
        step(s, 0, True)
    lax.fori_loop(returned + 1, last, step, 0)
    for p in range(PIECES):
        for d in range(2):
            block(d, p, last - 1).wait_recv()
    cross(last)
    for s in range(1, returned + 1):
        for d in range(2):
            back(d, s).wait_recv()
            here = columns(at(d, s))
            out_ref[d, 0, :, here] = back_in[d, s - 1, 0]
            out_ref[d, 1, :, here] = back_in[d, s - 1, 1]

    def drain(s, carry):
        for p in range(PIECES):
            for d in range(2):
                block(d, p, s).wait_send()
        return carry

    lax.fori_loop(0, last, drain, 0)
    for s in range(1, returned + 1):
        for d in range(2):
            back(d, s).wait_send()
    for copy in edges + rims[0] + rims[1]:
        copy.wait_send()


def body(n, m, spectra, taps):
    _, windows, bins, lanes = spectra.shape
    taps_count = taps.shape[1]
    returned = min(RETURNED, (n - 2) // 2)
    wide = pl.cdiv(taps.shape[0], lanes) * lanes
    bands = bins // BAND_BINS
    depth = 2 * windows * BAND_BINS
    vmem = pl.BlockSpec(memory_space=pltpu.VMEM)
    dma = pltpu.SemaphoreType.DMA
    return pl.pallas_call(
        partial(kernel, n, m, bins),
        out_shape=jax.ShapeDtypeStruct((bands, 2, lanes, n * lanes), BF16),
        in_specs=[pl.BlockSpec(memory_space=pltpu.HBM)] * 2,
        out_specs=vmem,
        scratch_shapes=[
            pltpu.VMEM((2, windows * bins, lanes), F32),
            pltpu.VMEM(taps.shape[::-1], F32),
            dma((3,)),
            pltpu.VMEM((taps_count, windows * bins // 2), F32),
            pltpu.VMEM((lanes, wide), F32),
            pltpu.VMEM((wide, lanes), F32),
            pltpu.VMEM((2, lanes + taps_count, windows * bins), F32),
            pltpu.VMEM((2, lanes, windows * bins), F32),
            pltpu.VMEM((2, windows * bins, lanes), F32),
            pltpu.VMEM((windows, bins + 16, lanes), F32),
            pltpu.VMEM((2, windows // 4, 8, lanes), F32),
            pltpu.VMEM((2, windows // 4, 8, lanes), F32),
            pltpu.VMEM((n - returned, bands, depth, lanes), BF16),
            pltpu.VMEM((bands, 2 * lanes, depth), BF16),
            pltpu.VMEM((2, returned, 2, lanes, lanes), BF16),
            pltpu.VMEM((2, returned, 2, lanes, lanes), BF16),
            dma((2,)),
            dma((2,)),
            dma((2, 2)),
            dma((2, 2)),
            dma((2, PIECES, n)),
            dma((2, PIECES, n)),
            dma((2, returned)),
            dma((2, returned)),
        ],
        compiler_params=pltpu.CompilerParams(
            collective_id=0, has_side_effects=True, vmem_limit_bytes=56 * 2**20
        ),
    )(spectra.reshape(2, windows * bins, lanes), taps.T)


def solution(mesh):
    placed = (P(None, None, "band", "chan"), P())
    return jax.shard_map(
        partial(body, mesh.shape["chan"], mesh.shape["band"]),
        mesh=mesh, in_specs=placed, out_specs=P("band", None, "chan", None), check_vma=False,
    )
```
